1024 devices in a mesh: mp: 16 (over y_hi, x, core), intra: 16 (over z), inter: 4 (over y_lo).
Axes of the slice: x: 4, y: 8 (y_hi: 2, y_lo: 4; y = y_hi * 4 + y_lo), z: 16, core: 2. Of those that a mesh axis runs over, the one named last changes fastest.
Arguments:
- activations: bfloat16 [32768, 512], P(('intra', 'inter'), 'mp'), may hold values from -16 to 16
- cotangent: bfloat16 [32768, 28672], P(('intra', 'inter'), 'mp'), may hold values from -0.03125 to 0.03125
Outputs:
- grad_bucket: float32 [512, 28672], P(('intra', 'inter'), 'mp')
The draws below stay inside these ranges and needn't reach their ends.
All inputs are finite; a program needn't handle non-finite values.
Results may differ from the reference program's by a relative error of at most 0.0041.
Values may be sent and summed in bfloat16 or wider, within the bound.
No kernel may reach another device: no remote copies, remote signals or barrier semaphores. Data moves between devices by JAX's collectives and lax.ppermute only.
A program may use at most 32 MiB of HBM per device.

```python
import jax
import jax.numpy as jnp
from jax import lax

FF = 28672
BUCKET = 512
TOK_DEV = 512
TOKENS = 32768
N_INTRA = 16
N_INTER = 4


def raised(array, stream_key, source, target, shards_of, factor):
    owner, partner = [(jnp.arange(array.shape[position]) // (array.shape[position] // shards_of)).reshape([-1 if axis == position else 1 for axis in range(array.ndim)]) for position in (source, target)]
    chosen = jax.random.permutation(stream_key, shards_of)[partner]
    strong = (owner == chosen) | (owner == (partner + shards_of // 2) % shards_of)
    return jnp.where(strong, factor * array, array)


def block_levels(own_key, shape, shards, low, largest):
    level, own = 1.0, jax.random.fold_in(own_key, 6)
    for axis_at, parts in shards:
        steps = jnp.exp(jax.random.uniform(jax.random.fold_in(own, axis_at), (parts,), jnp.float32, low / len(shards), largest / len(shards)))
        level = level * jnp.repeat(steps, shape[axis_at] // parts).reshape([-1 if axis == axis_at else 1 for axis in range(len(shape))])
    return level


def normal_values(key, dims, spread, limit, split=(), kind=jnp.bfloat16):
    factor_of = block_levels(key, dims, split, -0.22, 0.18) if split else 1.0
    array = jax.random.normal(key, dims, jnp.float32) * spread * factor_of
    return jnp.minimum(jnp.maximum(array, -limit), limit).astype(kind)


def noise_with(rng, extent, width, reach, shards, heavy, kind=jnp.bfloat16):
    drawn = width * jax.random.normal(rng, extent, jnp.float32)
    if shards:
        drawn = drawn * block_levels(rng, extent, shards, -0.22, 0.18)
    return jnp.clip(raised(drawn, jax.random.fold_in(rng, 3), *heavy), -reach, reach).astype(kind)


def setup_inputs(seed: int = 0) -> dict:
    keys = jax.random.split(jax.random.key(seed), 3)
    return {
        "activations": noise_with(keys[0], (TOKENS, BUCKET), 1.0, 16.0, ((0, 64), (1, 16)), (0, 1, 64, 4.0)),
        "cotangent": normal_values(keys[1], (TOKENS, FF), TOKENS ** -0.5, 0.03125, ((0, 64), (1, 16))),
    }


def reference(activations, cotangent):
    running = jnp.zeros((BUCKET, FF), jnp.float32)
    for outer_index in range(N_INTER):
        def accumulate(carry, inner_index):
            group_index = inner_index * N_INTER + outer_index
            row_start = (group_index * TOK_DEV).astype(jnp.int32)
            token_rows = lax.dynamic_slice_in_dim(activations, row_start, TOK_DEV, 0)
            cot_rows = lax.dynamic_slice_in_dim(cotangent, row_start, TOK_DEV, 0)
            partial_value = jnp.dot(token_rows.T, cot_rows, preferred_element_type=jnp.float32)
            rounded = lax.optimization_barrier(partial_value.astype(jnp.bfloat16))
            return carry + rounded.astype(jnp.float32), None

        inner_sum, unused = lax.scan(accumulate, jnp.zeros((BUCKET, FF), jnp.float32),
                                     jnp.arange(N_INTRA, dtype=jnp.int32))
        second_terms = lax.optimization_barrier(inner_sum.astype(jnp.bfloat16))
        running = running + second_terms.astype(jnp.float32)
    return running
```

```python
import jax
import jax.numpy as jnp
from jax import lax
from jax.sharding import PartitionSpec as P

BF = jnp.bfloat16
F32 = jnp.float32


def ring(size, step):
    return [(i, (i + step) % size) for i in range(size)]


def pairs(size):
    one = [(i, i ^ 1) for i in range(size)]
    other = [(i, (i - 1) % size if i % 2 == 0 else (i + 1) % size) for i in range(size)]
    return one, other


def rotated(blocks, shift, axis):
    doubled = jnp.concatenate([blocks, blocks], axis=axis)
    return lax.dynamic_slice_in_dim(doubled, shift, blocks.shape[axis], axis)


def product(rows, columns):
    return lax.dot_general(
        rows, columns, (((1,), (0,)), ((), ())), preferred_element_type=F32
    ).astype(BF)


def gathered(activations):
    size = lax.axis_size("mp")
    half = size // 2
    far = [[i, i + half] for i in range(half)]
    row = [[h * half + 2 * x + c for x in range(half // 2)] for h in range(2) for c in range(2)]
    chip = [[i, i + 1] for i in range(0, size, 2)]
    out = activations.T
    for groups in (far, row, chip):
        out = lax.all_gather(out, "mp", axis_index_groups=groups)
    out = out.transpose(2, 1, 0, 3, 4)
    return out.reshape(-1, out.shape[-1])


def shards(activations, cotangent):
    n, replicas = lax.axis_size("intra"), lax.axis_size("inter")
    z, y = lax.axis_index("intra"), lax.axis_index("inter")
    features = gathered(activations)
    tokens = features.shape[1]
    blocks = features.reshape(n // 2, 2, replicas, -1, tokens).transpose(1, 2, 0, 3, 4)
    blocks = rotated(rotated(blocks, z % 2, 0), y, 1)
    keep, give = (blocks[i].reshape(-1, tokens) for i in range(2))
    cols = cotangent.shape[1]
    half = cols // 2
    sums = []
    for part, perm in zip((cotangent[:, :half], cotangent[:, half:]), pairs(n)):
        other = lax.ppermute(product(give, part), "intra", perm)
        own = product(keep, part)
        sums.append((own.astype(F32) + other.astype(F32)).astype(BF))
    sums = jnp.concatenate(sums, axis=1).reshape(replicas, -1, cols)
    others = [lax.ppermute(sums[k], "inter", ring(replicas, k)) for k in range(1, replicas)]
    total = sums[0].astype(F32)
    for other in others:
        total = total + other.astype(F32)
    total = total.astype(BF).reshape(n // 2, -1, cols)
    total = lax.all_to_all(
        total, "intra", split_axis=0, concat_axis=0, tiled=True,
        axis_index_groups=[list(range(0, n, 2)), list(range(1, n, 2))],
    )
    return jnp.sum(total.astype(F32), axis=0)


def solution(mesh):
    return jax.shard_map(
        shards,
        mesh=mesh,
        in_specs=(P(("intra", "inter"), "mp"), P(("intra", "inter"), "mp")),
        out_specs=P(("intra", "inter"), "mp"),
        check_vma=False,
    )
```

```python
import jax
import jax.numpy as jnp
from jax import lax
from jax.sharding import PartitionSpec as P

BF = jnp.bfloat16
F32 = jnp.float32


def ring(size, step):
    return [(i, (i + step) % size) for i in range(size)]


def rotated(blocks, shift, axis):
    doubled = jnp.concatenate([blocks, blocks], axis=axis)
    return lax.dynamic_slice_in_dim(doubled, shift, blocks.shape[axis], axis)


def product(rows, columns):
    return lax.dot_general(
        rows, columns, (((1,), (0,)), ((), ())), preferred_element_type=F32
    ).astype(BF)


def gathered(activations):
    size = lax.axis_size("mp")
    chips = [[i for i in range(size) if i % 2 == core] for core in range(2)]
    pair = [[i, i + 1] for i in range(0, size, 2)]
    own = activations.T
    copies = jnp.broadcast_to(own[None], (size // 2,) + own.shape)
    half = lax.all_to_all(
        copies, "mp", split_axis=0, concat_axis=0, tiled=True, axis_index_groups=chips
    )
    both = lax.all_gather(half, "mp", axis_index_groups=pair)
    return both.swapaxes(0, 1).reshape(-1, own.shape[1])


def shards(activations, cotangent):
    n, replicas = lax.axis_size("intra"), lax.axis_size("inter")
    y = lax.axis_index("inter")
    features = gathered(activations)
    tokens = features.shape[1]
    cols = cotangent.shape[1]
    blocks = features.reshape(n, replicas, -1, tokens).transpose(1, 0, 2, 3)
    blocks = rotated(blocks, y, 0).reshape(replicas, -1, tokens)
    terms = [product(blocks[k], cotangent) for k in range(replicas)]
    others = [lax.ppermute(terms[k], "inter", ring(replicas, k)) for k in (2, 1, 3)]
    total = terms[0].astype(F32)
    for other in others:
        total = total + other.astype(F32)
    total = total.astype(BF).reshape(n, -1, cols)
    total = lax.all_to_all(total, "intra", split_axis=0, concat_axis=0, tiled=True)
    return jnp.sum(total.astype(F32), axis=0)


def solution(mesh):
    return jax.shard_map(
        shards,
        mesh=mesh,
        in_specs=(P(("intra", "inter"), "mp"), P(("intra", "inter"), "mp")),
        out_specs=P(("intra", "inter"), "mp"),
        check_vma=False,
    )
```

```python
import jax
import jax.numpy as jnp
from jax import lax
from jax.sharding import PartitionSpec as P

BF = jnp.bfloat16
F32 = jnp.float32


def ring(size, step):
    return [(i, (i + step) % size) for i in range(size)]


def rotated(blocks, shift, axis):
    doubled = jnp.concatenate([blocks, blocks], axis=axis)
    return lax.dynamic_slice_in_dim(doubled, shift, blocks.shape[axis], axis)


def product(rows, columns):
    return lax.dot_general(
        rows, columns, (((1,), (0,)), ((), ())), preferred_element_type=F32
    ).astype(BF)


def gathered(activations):
    size = lax.axis_size("mp")
    chips = [[i for i in range(size) if i % 2 == core] for core in range(2)]
    pair = [[i, i + 1] for i in range(0, size, 2)]
    own = activations.T
    copies = jnp.broadcast_to(own[None], (size // 2,) + own.shape)
    half = lax.all_to_all(
        copies, "mp", split_axis=0, concat_axis=0, tiled=True, axis_index_groups=chips
    )
    both = lax.all_gather(half, "mp", axis_index_groups=pair)
    return both.swapaxes(0, 1).reshape(-1, own.shape[1])


ROUNDS = (
    ((1, (1, 4, 7, -2, -5)), (-1, (-1, 2, 5, -4, -7)), (2, (8,))),
    ((3, (6,)), (-3, (-6,))),
    ((3, (3,)), (-3, (-3,))),
)
KEPT = (0, 3, -3, 6, -6)


def shards(activations, cotangent):
    n, replicas = lax.axis_size("intra"), lax.axis_size("inter")
    z = lax.axis_index("intra")
    features = gathered(activations)
    tokens = features.shape[1]
    cols = cotangent.shape[1]
    blocks = rotated(features.reshape(n, -1, tokens), z, 0)

    def terms(numbers):
        rows = jnp.concatenate([blocks[k % n] for k in numbers], axis=0)
        return product(rows, cotangent)

    sums = {}
    for moves in ROUNDS:
        if not sums:
            sent = [terms(numbers) for _, numbers in moves]
        else:
            sent = [
                jnp.concatenate([sums.pop(k).astype(BF) for k in numbers], axis=0)
                for _, numbers in moves
            ]
            sent = lax.optimization_barrier(sent)
        came = [lax.ppermute(x, "intra", ring(n, s)) for x, (s, _) in zip(sent, moves)]
        if not sums:
            own = terms(KEPT).reshape(len(KEPT), -1, cols).astype(F32)
            sums = {k: own[i] for i, k in enumerate(KEPT)}
        came = lax.optimization_barrier(came)
        for x, (s, numbers) in zip(came, moves):
            x = x.reshape(len(numbers), -1, cols).astype(F32)
            for i, k in enumerate(numbers):
                sums[k - s] = sums[k - s] + x[i]
    second = sums[0].astype(BF).reshape(replicas, -1, cols)
    second = lax.all_to_all(second, "inter", split_axis=0, concat_axis=0, tiled=True)
    return jnp.sum(second.astype(F32), axis=0)


def solution(mesh):
    return jax.shard_map(
        shards,
        mesh=mesh,
        in_specs=(P(("intra", "inter"), "mp"), P(("intra", "inter"), "mp")),
        out_specs=P(("intra", "inter"), "mp"),
        check_vma=False,
    )
```

```python
import jax
import jax.numpy as jnp
from jax import lax
from jax.sharding import PartitionSpec as P

BF = jnp.bfloat16
F32 = jnp.float32


def ring(size, step):
    return [(i, (i + step) % size) for i in range(size)]


def rotated(blocks, shift, axis):
    doubled = jnp.concatenate([blocks, blocks], axis=axis)
    return lax.dynamic_slice_in_dim(doubled, shift, blocks.shape[axis], axis)


def product(rows, columns):
    return lax.dot_general(
        rows, columns, (((1,), (0,)), ((), ())), preferred_element_type=F32
    ).astype(BF)


def gathered(activations):
    size = lax.axis_size("mp")
    chips = [[i for i in range(size) if i % 2 == core] for core in range(2)]
    pair = [[i, i + 1] for i in range(0, size, 2)]
    own = activations.T
    copies = jnp.broadcast_to(own[None], (size // 2,) + own.shape)
    half = lax.all_to_all(
        copies, "mp", split_axis=0, concat_axis=0, tiled=True, axis_index_groups=chips
    )
    both = lax.all_gather(half, "mp", axis_index_groups=pair)
    return both.swapaxes(0, 1).reshape(-1, own.shape[1])


ROUNDS = (
    ((1, (1, 4, 7, -2, -5)), (-1, (-1, 2, 5, -4, -7)), (2, (8,))),
    ((3, (6,)), (-3, (-6,))),
    ((3, (3,)), (-3, (-3,))),
)
KEPT = (0, 3, -3, 6, -6)


def moved(block, step):
    size, n = lax.axis_size("mp"), lax.axis_size("intra")
    perm = []
    for m in range(size):
        way = step if m % 2 == 0 else -step
        perm += [(m * n + z, m * n + (z + way) % n) for z in range(n)]
    return lax.ppermute(block, ("mp", "intra"), perm)


def reduced(features, cotangent):
    n, replicas = lax.axis_size("intra"), lax.axis_size("inter")
    z, core = lax.axis_index("intra"), lax.axis_index("mp") % 2
    tokens = features.shape[1]
    cols = cotangent.shape[1]
    blocks = features.reshape(n, -1, tokens)
    backward = jnp.concatenate([blocks[:1], blocks[:0:-1]], axis=0)
    blocks = jnp.where(core == 0, blocks, backward)
    blocks = rotated(blocks, jnp.where(core == 0, z, (n - z) % n), 0)

    def terms(numbers):
        rows = jnp.concatenate([blocks[k % n] for k in numbers], axis=0)
        return product(rows, cotangent)

    sums = {}
    for moves in ROUNDS:
        if not sums:
            sent = [terms(numbers) for _, numbers in moves]
        else:
            sent = [
                jnp.concatenate([sums.pop(k).astype(BF) for k in numbers], axis=0)
                for _, numbers in moves
            ]
            sent = lax.optimization_barrier(sent)
        came = [moved(x, s) for x, (s, _) in zip(sent, moves)]
        if not sums:
            own = terms(KEPT).reshape(len(KEPT), -1, cols).astype(F32)
            sums = {k: own[i] for i, k in enumerate(KEPT)}
        came = lax.optimization_barrier(came)
        for x, (s, numbers) in zip(came, moves):
            x = x.reshape(len(numbers), -1, cols).astype(F32)
            for i, k in enumerate(numbers):
                sums[k - s] = sums[k - s] + x[i]
    second = sums[0].astype(BF).reshape(replicas, -1, cols)
    second = lax.all_to_all(second, "inter", split_axis=0, concat_axis=0, tiled=True)
    return jnp.sum(second.astype(F32), axis=0)


def shards(activations, cotangent):
    return reduced(gathered(activations), cotangent)


def solution(mesh):
    return jax.shard_map(
        shards,
        mesh=mesh,
        in_specs=(P(("intra", "inter"), "mp"), P(("intra", "inter"), "mp")),
        out_specs=P(("intra", "inter"), "mp"),
        check_vma=False,
    )
```

```python
import jax
import jax.numpy as jnp
from jax import lax
from jax.sharding import PartitionSpec as P

BF = jnp.bfloat16
F32 = jnp.float32


def ring(size, step):
    return [(i, (i + step) % size) for i in range(size)]


def rotated(blocks, shift, axis):
    doubled = jnp.concatenate([blocks, blocks], axis=axis)
    return lax.dynamic_slice_in_dim(doubled, shift, blocks.shape[axis], axis)


def product(rows, columns):
    return lax.dot_general(
        rows, columns, (((1,), (0,)), ((), ())), preferred_element_type=F32
    ).astype(BF)


def gathered(activations):
    size = lax.axis_size("mp")
    chips = [[i for i in range(size) if i % 2 == core] for core in range(2)]
    pair = [[i, i + 1] for i in range(0, size, 2)]
    own = activations.T
    copies = jnp.broadcast_to(own[None], (size // 2,) + own.shape)
    half = lax.all_to_all(
        copies, "mp", split_axis=0, concat_axis=0, tiled=True, axis_index_groups=chips
    )
    both = lax.all_gather(half, "mp", axis_index_groups=pair)
    return both.swapaxes(0, 1).reshape(-1, own.shape[1])


ROUNDS = (
    ((1, (1, 5, 8, -2, -5)), (-1, (-1, 2, 6, -4, -7))),
    ((3, (3, 7)), (-3, (-6,))),
    ((4, (4,)), (-3, (-3,))),
)
KEPT = (0, 3, 4, 7, -3, -6)


def moved(block, step):
    size, n = lax.axis_size("mp"), lax.axis_size("intra")
    perm = []
    for m in range(size):
        way = step if m % 2 == 0 else -step
        perm += [(m * n + z, m * n + (z + way) % n) for z in range(n)]
    return lax.ppermute(block, ("mp", "intra"), perm)


def reduced(features, cotangent):
    n, replicas = lax.axis_size("intra"), lax.axis_size("inter")
    z, core = lax.axis_index("intra"), lax.axis_index("mp") % 2
    tokens = features.shape[1]
    cols = cotangent.shape[1]
    blocks = features.reshape(n, -1, tokens)
    backward = jnp.concatenate([blocks[:1], blocks[:0:-1]], axis=0)
    blocks = jnp.where(core == 0, blocks, backward)
    blocks = rotated(blocks, jnp.where(core == 0, z, (n - z) % n), 0)

    def terms(numbers):
        rows = jnp.concatenate([blocks[k % n] for k in numbers], axis=0)
        return product(rows, cotangent)

    sums = {}
    for moves in ROUNDS:
        if not sums:
            sent = [terms(numbers) for _, numbers in moves]
        else:
            sent = [
                jnp.concatenate([sums.pop(k).astype(BF) for k in numbers], axis=0)
                for _, numbers in moves
            ]
            sent = lax.optimization_barrier(sent)
        came = [moved(x, s) for x, (s, _) in zip(sent, moves)]
        if not sums:
            own = terms(KEPT).reshape(len(KEPT), -1, cols).astype(F32)
            sums = {k: own[i] for i, k in enumerate(KEPT)}
        came = lax.optimization_barrier(came)
        for x, (s, numbers) in zip(came, moves):
            x = x.reshape(len(numbers), -1, cols).astype(F32)
            for i, k in enumerate(numbers):
                sums[k - s] = sums[k - s] + x[i]
    second = sums[0].astype(BF).reshape(replicas, -1, cols)
    second = lax.all_to_all(second, "inter", split_axis=0, concat_axis=0, tiled=True)
    return jnp.sum(second.astype(F32), axis=0)


def shards(activations, cotangent):
    return reduced(gathered(activations), cotangent)


def solution(mesh):
    return jax.shard_map(
        shards,
        mesh=mesh,
        in_specs=(P(("intra", "inter"), "mp"), P(("intra", "inter"), "mp")),
        out_specs=P(("intra", "inter"), "mp"),
        check_vma=False,
    )
```

```python
import jax
import jax.numpy as jnp
from jax import lax
from jax.sharding import PartitionSpec as P

BF = jnp.bfloat16
F32 = jnp.float32


def ring(size, step):
    return [(i, (i + step) % size) for i in range(size)]


def rotated(blocks, shift, axis):
    doubled = jnp.concatenate([blocks, blocks], axis=axis)
    return lax.dynamic_slice_in_dim(doubled, shift, blocks.shape[axis], axis)


def product(rows, columns):
    return lax.dot_general(
        rows, columns, (((1,), (0,)), ((), ())), preferred_element_type=F32
    ).astype(BF)


def gathered(activations):
    size = lax.axis_size("mp")
    half = size // 2
    far = [[i, i + half] for i in range(half)]
    line = [[f * half + i + c for i in range(0, half, 2)] for f in range(2) for c in range(2)]
    pair = [[i, i + 1] for i in range(0, size, 2)]
    own = activations.T
    out = lax.all_gather(own, "mp", axis_index_groups=far)
    out = jnp.broadcast_to(out[None], (half // 2,) + out.shape)
    out = lax.all_to_all(
        out, "mp", split_axis=0, concat_axis=0, tiled=True, axis_index_groups=line
    )
    out = lax.all_gather(out, "mp", axis_index_groups=pair)
    return out.transpose(2, 1, 0, 3, 4).reshape(-1, own.shape[1])


ROUNDS = (
    ((1, (1, 5, 8, -2, -5)), (-1, (-1, 2, 6, -4, -7))),
    ((3, (3, 7)), (-3, (-6,))),
    ((4, (4,)), (-3, (-3,))),
)
KEPT = (0, 3, 4, 7, -3, -6)


def moved(block, step):
    size, n = lax.axis_size("mp"), lax.axis_size("intra")
    perm = []
    for m in range(size):
        way = step if m % 2 == 0 else -step
        perm += [(m * n + z, m * n + (z + way) % n) for z in range(n)]
    return lax.ppermute(block, ("mp", "intra"), perm)


def reduced(features, cotangent):
    n, replicas = lax.axis_size("intra"), lax.axis_size("inter")
    z, core = lax.axis_index("intra"), lax.axis_index("mp") % 2
    tokens = features.shape[1]
    cols = cotangent.shape[1]
    blocks = features.reshape(n, -1, tokens)
    backward = jnp.concatenate([blocks[:1], blocks[:0:-1]], axis=0)
    blocks = jnp.where(core == 0, blocks, backward)
    blocks = rotated(blocks, jnp.where(core == 0, z, (n - z) % n), 0)

    def terms(numbers):
        rows = jnp.concatenate([blocks[k % n] for k in numbers], axis=0)
        return product(rows, cotangent)

    sums = {}
    for moves in ROUNDS:
        if not sums:
            sent = [terms(numbers) for _, numbers in moves]
        else:
            sent = [
                jnp.concatenate([sums.pop(k).astype(BF) for k in numbers], axis=0)
                for _, numbers in moves
            ]
            sent = lax.optimization_barrier(sent)
        came = [moved(x, s) for x, (s, _) in zip(sent, moves)]
        if not sums:
            own = terms(KEPT).reshape(len(KEPT), -1, cols).astype(F32)
            sums = {k: own[i] for i, k in enumerate(KEPT)}
        came = lax.optimization_barrier(came)
        for x, (s, numbers) in zip(came, moves):
            x = x.reshape(len(numbers), -1, cols).astype(F32)
            for i, k in enumerate(numbers):
                sums[k - s] = sums[k - s] + x[i]
    second = sums[0].astype(BF).reshape(replicas, -1, cols)
    second = lax.all_to_all(second, "inter", split_axis=0, concat_axis=0, tiled=True)
    return jnp.sum(second.astype(F32), axis=0)


def shards(activations, cotangent):
    return reduced(gathered(activations), cotangent)


def solution(mesh):
    return jax.shard_map(
        shards,
        mesh=mesh,
        in_specs=(P(("intra", "inter"), "mp"), P(("intra", "inter"), "mp")),
        out_specs=P(("intra", "inter"), "mp"),
        check_vma=False,
    )
```

```python
import jax
import jax.numpy as jnp
from jax import lax
from jax.sharding import PartitionSpec as P

BF = jnp.bfloat16
F32 = jnp.float32


def ring(size, step):
    return [(i, (i + step) % size) for i in range(size)]


def rotated(blocks, shift, axis):
    doubled = jnp.concatenate([blocks, blocks], axis=axis)
    return lax.dynamic_slice_in_dim(doubled, shift, blocks.shape[axis], axis)


def product(rows, columns):
    return lax.dot_general(
        rows, columns, (((1,), (0,)), ((), ())), preferred_element_type=F32
    ).astype(BF)


def gathered(activations):
    size = lax.axis_size("mp")
    half = size // 2
    far = [[i, i + half] for i in range(half)]
    line = [[f * half + i + c for i in range(0, half, 2)] for f in range(2) for c in range(2)]
    pair = [[i, i + 1] for i in range(0, size, 2)]
    own = activations.T
    out = lax.all_gather(own, "mp", axis_index_groups=far)
    out = jnp.broadcast_to(out[None], (half // 2,) + out.shape)
    out = lax.all_to_all(
        out, "mp", split_axis=0, concat_axis=0, tiled=True, axis_index_groups=line
    )
    out = lax.all_gather(out, "mp", axis_index_groups=pair)
    return out.transpose(2, 1, 0, 3, 4).reshape(-1, own.shape[1])


ROUNDS = (
    ((3, (8,)), (2, (2, 7, -3)), (-2, (-2, 3, -7)), (1, (1, 6, -4)), (-1, (-1, 4, -6))),
    ((5, (5,)), (-5, (-5,))),
)
KEPT = (0, 5, -5)


def moved(block, step):
    size, n = lax.axis_size("mp"), lax.axis_size("intra")
    perm = []
    for m in range(size):
        way = step if m % 2 == 0 else -step
        perm += [(m * n + z, m * n + (z + way) % n) for z in range(n)]
    return lax.ppermute(block, ("mp", "intra"), perm)


def reduced(features, cotangent):
    n, replicas = lax.axis_size("intra"), lax.axis_size("inter")
    z, core = lax.axis_index("intra"), lax.axis_index("mp") % 2
    tokens = features.shape[1]
    cols = cotangent.shape[1]
    blocks = features.reshape(n, -1, tokens)
    backward = jnp.concatenate([blocks[:1], blocks[:0:-1]], axis=0)
    blocks = jnp.where(core == 0, blocks, backward)
    blocks = rotated(blocks, jnp.where(core == 0, z, (n - z) % n), 0)

    def terms(numbers):
        rows = jnp.concatenate([blocks[k % n] for k in numbers], axis=0)
        return product(rows, cotangent)

    sums = {}
    for moves in ROUNDS:
        if not sums:
            sent = [terms(numbers) for _, numbers in moves]
        else:
            sent = [
                jnp.concatenate([sums.pop(k).astype(BF) for k in numbers], axis=0)
                for _, numbers in moves
            ]
            sent = lax.optimization_barrier(sent)
        came = [moved(x, s) for x, (s, _) in zip(sent, moves)]
        if not sums:
            own = terms(KEPT).reshape(len(KEPT), -1, cols).astype(F32)
            sums = {k: own[i] for i, k in enumerate(KEPT)}
        came = lax.optimization_barrier(came)
        for x, (s, numbers) in zip(came, moves):
            x = x.reshape(len(numbers), -1, cols).astype(F32)
            for i, k in enumerate(numbers):
                sums[k - s] = sums[k - s] + x[i]
    second = sums[0].astype(BF).reshape(replicas, -1, cols)
    second = lax.all_to_all(second, "inter", split_axis=0, concat_axis=0, tiled=True)
    return jnp.sum(second.astype(F32), axis=0)


def shards(activations, cotangent):
    return reduced(gathered(activations), cotangent)


def solution(mesh):
    return jax.shard_map(
        shards,
        mesh=mesh,
        in_specs=(P(("intra", "inter"), "mp"), P(("intra", "inter"), "mp")),
        out_specs=P(("intra", "inter"), "mp"),
        check_vma=False,
    )
```

```python
import jax
import jax.numpy as jnp
from jax import lax
from jax.sharding import PartitionSpec as P

BF = jnp.bfloat16
F32 = jnp.float32


def ring(size, step):
    return [(i, (i + step) % size) for i in range(size)]


def rotated(blocks, shift, axis):
    doubled = jnp.concatenate([blocks, blocks], axis=axis)
    return lax.dynamic_slice_in_dim(doubled, shift, blocks.shape[axis], axis)


def product(rows, columns):
    return lax.dot_general(
        rows, columns, (((1,), (0,)), ((), ())), preferred_element_type=F32
    ).astype(BF)


def gathered(activations):
    size = lax.axis_size("mp")
    half = size // 2
    far = [[i, i + half] for i in range(half)]
    line = [[f * half + i + c for i in range(0, half, 2)] for f in range(2) for c in range(2)]
    pair = [[i, i + 1] for i in range(0, size, 2)]
    own = activations.T
    out = lax.all_gather(own, "mp", axis_index_groups=far)
    out = jnp.broadcast_to(out[None], (half // 2,) + out.shape)
    out = lax.all_to_all(
        out, "mp", split_axis=0, concat_axis=0, tiled=True, axis_index_groups=line
    )
    out = lax.all_gather(out, "mp", axis_index_groups=pair)
    return out.transpose(2, 1, 0, 3, 4).reshape(-1, own.shape[1])


ROUNDS = (
    ((1, (1, 4, 7, -2, -5)), (-1, (-1, 2, 5, -4, -7)), (2, (8,))),
    ((3, (6,)), (-3, (-6,))),
    ((3, (3,)), (-3, (-3,))),
)
KEPT = (0, 3, -3, 6, -6)


def moved(block, step):
    size, n = lax.axis_size("mp"), lax.axis_size("intra")
    perm = []
    for m in range(size):
        way = step if m % 2 == 0 else -step
        perm += [(m * n + z, m * n + (z + way) % n) for z in range(n)]
    return lax.ppermute(block, ("mp", "intra"), perm)


def reduced(features, cotangent):
    n, replicas = lax.axis_size("intra"), lax.axis_size("inter")
    z, core = lax.axis_index("intra"), lax.axis_index("mp") % 2
    tokens = features.shape[1]
    cols = cotangent.shape[1]
    blocks = features.reshape(n, -1, tokens)
    backward = jnp.concatenate([blocks[:1], blocks[:0:-1]], axis=0)
    blocks = jnp.where(core == 0, blocks, backward)
    blocks = rotated(blocks, jnp.where(core == 0, z, (n - z) % n), 0)

    def terms(numbers):
        rows = jnp.concatenate([blocks[k % n] for k in numbers], axis=0)
        return product(rows, cotangent)

    sums = {}
    for moves in ROUNDS:
        if not sums:
            sent = [terms(numbers) for _, numbers in moves]
        else:
            sent = [
                jnp.concatenate([sums.pop(k).astype(BF) for k in numbers], axis=0)
                for _, numbers in moves
            ]
            sent = lax.optimization_barrier(sent)
        came = [moved(x, s) for x, (s, _) in zip(sent, moves)]
        if not sums:
            own = terms(KEPT).reshape(len(KEPT), -1, cols).astype(F32)
            sums = {k: own[i] for i, k in enumerate(KEPT)}
        came = lax.optimization_barrier(came)
        for x, (s, numbers) in zip(came, moves):
            x = x.reshape(len(numbers), -1, cols).astype(F32)
            for i, k in enumerate(numbers):
                sums[k - s] = sums[k - s] + x[i]
    second = sums[0].astype(BF).reshape(replicas, -1, cols)
    second = lax.all_to_all(second, "inter", split_axis=0, concat_axis=0, tiled=True)
    return jnp.sum(second.astype(F32), axis=0)


def shards(activations, cotangent):
    return reduced(gathered(activations), cotangent)


def solution(mesh):
    return jax.shard_map(
        shards,
        mesh=mesh,
        in_specs=(P(("intra", "inter"), "mp"), P(("intra", "inter"), "mp")),
        out_specs=P(("intra", "inter"), "mp"),
        check_vma=False,
    )
```

```python
import jax
import jax.numpy as jnp
from jax import lax
from jax.sharding import PartitionSpec as P

BF = jnp.bfloat16
F32 = jnp.float32


def ring(size, step):
    return [(i, (i + step) % size) for i in range(size)]


def rotated(blocks, shift, axis):
    doubled = jnp.concatenate([blocks, blocks], axis=axis)
    return lax.dynamic_slice_in_dim(doubled, shift, blocks.shape[axis], axis)


def product(rows, columns):
    return lax.dot_general(
        rows, columns, (((1,), (0,)), ((), ())), preferred_element_type=F32
    ).astype(BF)


def gathered(activations):
    size = lax.axis_size("mp")
    half = size // 2
    far = [[i, i + half] for i in range(half)]
    line = [[f * half + i + c for i in range(0, half, 2)] for f in range(2) for c in range(2)]
    pair = [[i, i + 1] for i in range(0, size, 2)]
    own = activations.T
    out = lax.all_gather(own, "mp", axis_index_groups=far)
    out = jnp.broadcast_to(out[None], (half // 2,) + out.shape)
    out = lax.all_to_all(
        out, "mp", split_axis=0, concat_axis=0, tiled=True, axis_index_groups=line
    )
    out = lax.all_gather(out, "mp", axis_index_groups=pair)
    return out.transpose(2, 1, 0, 3, 4).reshape(-1, own.shape[1])


ROUNDS = (
    ((1, (1, 5, 8, -2, -5)), (-1, (-1, 2, 6, -4, -7))),
    ((3, (3, 7)), (-3, (-6,))),
    ((4, (4,)), (-3, (-3,))),
)
KEPT = (0, 3, 4, 7, -3, -6)


def moved(block, step):
    size, n = lax.axis_size("mp"), lax.axis_size("intra")
    perm = []
    for m in range(size):
        way = step if m % 2 == 0 else -step
        perm += [(m * n + z, m * n + (z + way) % n) for z in range(n)]
    return lax.ppermute(block, ("mp", "intra"), perm)


def reduced(features, cotangent, z, core):
    n, replicas = lax.axis_size("intra"), lax.axis_size("inter")
    tokens = features.shape[1]
    cols = cotangent.shape[1]
    blocks = features.reshape(n, -1, tokens)
    backward = jnp.concatenate([blocks[:1], blocks[:0:-1]], axis=0)
    blocks = jnp.where(core == 0, blocks, backward)
    blocks = rotated(blocks, jnp.where(core == 0, z, (n - z) % n), 0)

    def terms(numbers):
        rows = jnp.concatenate([blocks[k % n] for k in numbers], axis=0)
        return product(rows, cotangent)

    sums = {}
    for moves in ROUNDS:
        if not sums:
            sent = [terms(numbers) for _, numbers in moves]
        else:
            sent = [
                jnp.concatenate([sums.pop(k).astype(BF) for k in numbers], axis=0)
                for _, numbers in moves
            ]
            sent = lax.optimization_barrier(sent)
        came = [moved(x, s) for x, (s, _) in zip(sent, moves)]
        if not sums:
            own = terms(KEPT).reshape(len(KEPT), -1, cols).astype(F32)
            sums = {k: own[i] for i, k in enumerate(KEPT)}
        came = lax.optimization_barrier(came)
        for x, (s, numbers) in zip(came, moves):
            x = x.reshape(len(numbers), -1, cols).astype(F32)
            for i, k in enumerate(numbers):
                sums[k - s] = sums[k - s] + x[i]
    second = sums[0].astype(BF).reshape(replicas, -1, cols)
    second = lax.all_to_all(second, "inter", split_axis=0, concat_axis=0, tiled=True)
    return jnp.sum(second.astype(F32), axis=0)


def shards(activations, cotangent):
    z, core = lax.axis_index("intra"), lax.axis_index("mp") % 2
    activations, z, core = lax.optimization_barrier((activations, z, core))
    features, z, core = lax.optimization_barrier((gathered(activations), z, core))
    return reduced(features, cotangent, z, core)


def solution(mesh):
    return jax.shard_map(
        shards,
        mesh=mesh,
        in_specs=(P(("intra", "inter"), "mp"), P(("intra", "inter"), "mp")),
        out_specs=P(("intra", "inter"), "mp"),
        check_vma=False,
    )
```

```python
import jax
import jax.numpy as jnp
from jax import lax
from jax.sharding import PartitionSpec as P

BF = jnp.bfloat16
F32 = jnp.float32


def ring(size, step):
    return [(i, (i + step) % size) for i in range(size)]


def rotated(blocks, shift, axis):
    doubled = jnp.concatenate([blocks, blocks], axis=axis)
    return lax.dynamic_slice_in_dim(doubled, shift, blocks.shape[axis], axis)


def product(rows, columns):
    return lax.dot_general(
        rows, columns, (((1,), (0,)), ((), ())), preferred_element_type=F32
    ).astype(BF)


def gathered(activations):
    size = lax.axis_size("mp")
    chips = [[i for i in range(size) if i % 2 == core] for core in range(2)]
    pair = [[i, i + 1] for i in range(0, size, 2)]
    own = activations.T
    copies = jnp.broadcast_to(own[None], (size // 2,) + own.shape)
    half = lax.all_to_all(
        copies, "mp", split_axis=0, concat_axis=0, tiled=True, axis_index_groups=chips
    )
    both = lax.all_gather(half, "mp", axis_index_groups=pair)
    return both.swapaxes(0, 1).reshape(-1, own.shape[1])


ROUNDS = (
    ((1, (1, 5, 8, -2, -5)), (-1, (-1, 2, 6, -4, -7))),
    ((3, (3, 7)), (-3, (-6,))),
    ((4, (4,)), (-3, (-3,))),
)
KEPT = (0, 3, 4, 7, -3, -6)


def moved(block, step):
    size, n = lax.axis_size("mp"), lax.axis_size("intra")
    perm = []
    for m in range(size):
        way = step if m % 2 == 0 else -step
        perm += [(m * n + z, m * n + (z + way) % n) for z in range(n)]
    return lax.ppermute(block, ("mp", "intra"), perm)


def reduced(features, cotangent, z, core):
    n, replicas = lax.axis_size("intra"), lax.axis_size("inter")
    tokens = features.shape[1]
    cols = cotangent.shape[1]
    blocks = features.reshape(n, -1, tokens)
    backward = jnp.concatenate([blocks[:1], blocks[:0:-1]], axis=0)
    blocks = jnp.where(core == 0, blocks, backward)
    blocks = rotated(blocks, jnp.where(core == 0, z, (n - z) % n), 0)

    def terms(numbers):
        rows = jnp.concatenate([blocks[k % n] for k in numbers], axis=0)
        return product(rows, cotangent)

    sums = {}
    for moves in ROUNDS:
        if not sums:
            sent = [terms(numbers) for _, numbers in moves]
        else:
            sent = [
                jnp.concatenate([sums.pop(k).astype(BF) for k in numbers], axis=0)
                for _, numbers in moves
            ]
            sent = lax.optimization_barrier(sent)
        came = [moved(x, s) for x, (s, _) in zip(sent, moves)]
        if not sums:
            own = terms(KEPT).reshape(len(KEPT), -1, cols).astype(F32)
            sums = {k: own[i] for i, k in enumerate(KEPT)}
        came = lax.optimization_barrier(came)
        for x, (s, numbers) in zip(came, moves):
            x = x.reshape(len(numbers), -1, cols).astype(F32)
            for i, k in enumerate(numbers):
                sums[k - s] = sums[k - s] + x[i]
    second = sums[0].astype(BF).reshape(replicas, -1, cols)
    second = lax.all_to_all(second, "inter", split_axis=0, concat_axis=0, tiled=True)
    return jnp.sum(second.astype(F32), axis=0)


def shards(activations, cotangent):
    z, core = lax.axis_index("intra"), lax.axis_index("mp") % 2
    activations, z, core = lax.optimization_barrier((activations, z, core))
    features, z, core = lax.optimization_barrier((gathered(activations), z, core))
    return reduced(features, cotangent, z, core)


def solution(mesh):
    return jax.shard_map(
        shards,
        mesh=mesh,
        in_specs=(P(("intra", "inter"), "mp"), P(("intra", "inter"), "mp")),
        out_specs=P(("intra", "inter"), "mp"),
        check_vma=False,
    )
```
